512 devices in a mesh: grp: 4 (over x), seq: 32 (over y_lo, z), rep: 4 (over y_hi, core).
Axes of the slice: x: 4, y: 8 (y_hi: 2, y_lo: 4; y = y_hi * 4 + y_lo), z: 8, core: 2. Of those that a mesh axis runs over, the one named last changes fastest.
Arguments:
- feature: bfloat16 [4, 4096, 16384], P('rep', None, ('grp', 'seq')), may hold values from -0.0234375 to 0.0234375
- cotangent: bfloat16 [4, 4096, 16384], P('rep', None, ('grp', 'seq')), may hold values from -6 to 6
- long_filter: bfloat16 [4096, 16384], P(None, ('grp', 'seq')), may hold values from -1 to 1
- short_filter: float32 [4096, 3], replicated, may hold values from -3 to 3
- skip_gain: float32 [4096], replicated, may hold values from -1 to 1
Outputs:
- input_grad: bfloat16 [4, 4096, 16384], P('rep', None, ('grp', 'seq'))
- filter_grad: float32 [4096, 16384], P('rep', ('grp', 'seq'))
- skip_grad: float32 [4096], replicated
The draws below stay inside these ranges and needn't reach their ends.
All inputs are finite; a program needn't handle non-finite values.
Results may differ from the reference program's by a relative error of at most 0.012.
Values may be sent and summed in bfloat16 or wider, within the bound.
A program may use at most 64 MiB of HBM per device.

```python
import math
import jax
import jax.numpy as jnp
from jax import lax

CH = 4096
SHARD_LEN = 128
TAPS = 3
SHARDS = 128
SEQ_LEN = 16384
REPLICAS = 4


def draw_long_filter(key, part):
    key = jax.random.fold_in(key, 7)
    key_mask, key_short, key_long, key_noise = jax.random.split(key, 4)
    quick_mask = jax.random.uniform(key_mask, (CH, 1)) < 0.5
    noise_draw = jnp.clip(jax.random.normal(key_noise, (CH, SEQ_LEN)), -5.0, 5.0)
    short_reach = jnp.exp(jax.random.uniform(key_short, (CH, 1), minval=jnp.log(30.0), maxval=jnp.log(50.0)))
    long_reach = SEQ_LEN * jnp.exp(jax.random.uniform(key_long, (CH, 1), minval=jnp.log(0.5), maxval=jnp.log(4.0)))
    reach_len = jnp.where(quick_mask, short_reach, long_reach)
    places = jnp.arange(SEQ_LEN, dtype=jnp.float32)[None, :]
    envelope = jnp.exp(-places / reach_len) / jnp.sqrt(jnp.minimum(reach_len, SEQ_LEN * 1.0))
    return (noise_draw * envelope).astype(jnp.bfloat16)


def steps_of(rng, dims, cuts, smallest, high):
    def one(position, parts):
        steps = jax.random.uniform(jax.random.fold_in(jax.random.fold_in(rng, 6), position), (parts,), jnp.float32, smallest / len(cuts), high / len(cuts))
        return jnp.repeat(jnp.exp(steps), dims[position] // parts).reshape((-1,) + (1,) * (len(dims) - position - 1))

    gain = one(*cuts[0])
    for cut in cuts[1:]:
        gain = gain * one(*cut)
    return gain


def centred(rng, extent, width, limit, cuts=(), held_as=jnp.bfloat16):
    values = jax.random.normal(rng, extent, jnp.float32) * width
    if len(cuts) > 0:
        values = steps_of(rng, extent, cuts, -0.22, 0.18) * values
    return jnp.clip(values, min=-limit, max=limit).astype(held_as)


def setup_inputs(seed: int = 0) -> dict:
    arg_keys = jax.random.split(jax.random.key(seed), 6)
    return {
        "feature": centred(arg_keys[0], (REPLICAS, CH, SEQ_LEN), (REPLICAS * SEQ_LEN) ** -0.5, 0.0234375, ((0, 4), (2, 128))),
        "cotangent": centred(arg_keys[1], (REPLICAS, CH, SEQ_LEN), 1.0, 6.0, ((0, 4), (2, 128))),
        "long_filter": draw_long_filter(jax.random.fold_in(arg_keys[5], 71), 0),
        "short_filter": centred(arg_keys[3], (CH, TAPS), 0.6, 3.0, (), jnp.float32),
        "skip_gain": jnp.clip(jax.random.uniform(arg_keys[4], (CH,), jnp.float32, -1.0, 1.0), -1.0, 1.0),
    }


def contract(pattern, left_side, right_side):
    return jnp.einsum(pattern, left_side.astype(jnp.float32), right_side.astype(jnp.float32), precision=lax.Precision.HIGHEST)


def spectral_tables(shards, shard_len):
    double = 2 * shards
    spectrum = double * shard_len
    freq_outer = jnp.arange(double, dtype=jnp.int32)[:, None]
    pos_outer = jnp.arange(shards, dtype=jnp.int32)[None, :]
    angle_outer = ((freq_outer * pos_outer) % double).astype(jnp.float32) * (-2.0 * math.pi / double)
    pos_inner = jnp.arange(shard_len, dtype=jnp.int32)
    angle_inner = ((pos_inner[:, None] * pos_inner[None, :]) % shard_len).astype(jnp.float32) * (-2.0 * math.pi / shard_len)
    angle_twist = ((freq_outer * pos_inner[None, :]) % spectrum).astype(jnp.float32) * (-2.0 * math.pi / spectrum)
    return (jnp.cos(angle_outer).astype(jnp.bfloat16), jnp.sin(angle_outer).astype(jnp.bfloat16),
            jnp.cos(angle_inner).astype(jnp.bfloat16), jnp.sin(angle_inner).astype(jnp.bfloat16),
            jnp.cos(angle_twist), jnp.sin(angle_twist))


def finish_forward(section_re, section_im, tables):
    outer_re, outer_im, inner_re, inner_im, twist_re, twist_im = tables
    bend_re = twist_re[:, None, :]
    bend_im = twist_im[:, None, :]
    turned_re = (section_re * bend_re - section_im * bend_im).astype(jnp.bfloat16)
    turned_im = (section_re * bend_im + section_im * bend_re).astype(jnp.bfloat16)
    spec_re = contract("gcm,mk->ckg", turned_re, inner_re) - contract("gcm,mk->ckg", turned_im, inner_im)
    spec_im = contract("gcm,mk->ckg", turned_re, inner_im) + contract("gcm,mk->ckg", turned_im, inner_re)
    rows_count = spec_re.shape[0]
    return spec_re.reshape(rows_count, -1), spec_im.reshape(rows_count, -1)


def spectrum_real(signal, tables):
    section_re = contract("gj,jcm->gcm", tables[0], signal)
    section_im = contract("gj,jcm->gcm", tables[1], signal)
    return finish_forward(section_re, section_im, tables)


def spectrum_complex(signal_re, signal_im, tables):
    section_re = contract("gj,jcm->gcm", tables[0], signal_re) - contract("gj,jcm->gcm", tables[1], signal_im)
    section_im = contract("gj,jcm->gcm", tables[1], signal_re) + contract("gj,jcm->gcm", tables[0], signal_im)
    return finish_forward(section_re, section_im, tables)


def mirrored(flat_spec):
    return jnp.roll(jnp.flip(flat_spec, 1), 1, 1)


def block_backward(feat_blk, cot_blk, filt_blk, tables):
    outer_re, outer_im, inner_re, inner_im, twist_re, twist_im = tables
    pack_re, pack_im = spectrum_complex(filt_blk, feat_blk, tables)
    mirror_re = mirrored(pack_re)
    mirror_im = mirrored(pack_im)
    filt_re = 0.5 * (pack_re + mirror_re)
    filt_im = 0.5 * (pack_im - mirror_im)
    feat_re = 0.5 * (pack_im + mirror_im)
    feat_im = 0.5 * (mirror_re - pack_re)
    cot_re, cot_im = spectrum_real(cot_blk, tables)
    join_re = filt_re * cot_re + filt_im * cot_im - (cot_im * feat_re - cot_re * feat_im)
    join_im = filt_re * cot_im - filt_im * cot_re + (cot_re * feat_re + cot_im * feat_im)
    grid_shape = (join_re.shape[0], inner_re.shape[0], outer_re.shape[0])
    join_re = join_re.astype(jnp.bfloat16).reshape(grid_shape)
    join_im = join_im.astype(jnp.bfloat16).reshape(grid_shape)
    back_re = contract("ckg,mk->gcm", join_re, inner_re) + contract("ckg,mk->gcm", join_im, inner_im)
    back_im = contract("ckg,mk->gcm", join_im, inner_re) - contract("ckg,mk->gcm", join_re, inner_im)
    bend_re = twist_re[:, None, :]
    bend_im = twist_im[:, None, :]
    turned_re = (back_re * bend_re + back_im * bend_im).astype(jnp.bfloat16)
    turned_im = (back_im * bend_re - back_re * bend_im).astype(jnp.bfloat16)
    out_re = contract("gj,gcm->jcm", outer_re, turned_re) + contract("gj,gcm->jcm", outer_im, turned_im)
    out_im = contract("gj,gcm->jcm", outer_re, turned_im) - contract("gj,gcm->jcm", outer_im, turned_re)
    inverse_scale = 1.0 / (outer_re.shape[0] * inner_re.shape[0])
    return (out_re * inverse_scale).astype(jnp.bfloat16), (out_im * inverse_scale).astype(jnp.bfloat16)


def reference(feature, cotangent, long_filter, short_filter, skip_gain):
    tables = spectral_tables(SHARDS, SHARD_LEN)
    block_width = 64
    blocks = CH // block_width

    def to_blocks(tensor):
        return tensor.reshape(block_width, SHARDS, SHARD_LEN).transpose(1, 0, 2)

    def from_blocks(tensor):
        return tensor.transpose(1, 0, 2).reshape(block_width, SEQ_LEN)

    def one_block(pieces):
        feat_blk, cot_blk, filt_blk = pieces
        longpart, filter_part = block_backward(to_blocks(feat_blk), to_blocks(cot_blk), to_blocks(filt_blk), tables)
        return from_blocks(longpart), from_blocks(filter_part)

    filt_split = long_filter.reshape(blocks, block_width, SEQ_LEN)

    def one_sequence(pieces):
        feat_seq, cot_seq = pieces
        return lax.map(one_block, (feat_seq.reshape(blocks, block_width, SEQ_LEN), cot_seq.reshape(blocks, block_width, SEQ_LEN), filt_split))

    longpart, filter_part = lax.map(one_sequence, (feature, cotangent))
    longpart = longpart.reshape(REPLICAS, CH, SEQ_LEN)
    filter_part = filter_part.reshape(REPLICAS, CH, SEQ_LEN)
    filter_grad = jnp.sum(filter_part.astype(jnp.float32), axis=0)
    total_grad = longpart.astype(jnp.float32) + skip_gain[None, :, None] * cotangent.astype(jnp.float32)
    extended = jnp.concatenate([total_grad, jnp.zeros((REPLICAS, CH, TAPS - 1), jnp.float32)], axis=2)
    input_grad = short_filter[None, :, 0:1] * total_grad
    for offset in range(1, TAPS):
        input_grad = input_grad + short_filter[None, :, offset:offset + 1] * extended[:, :, offset:offset + SEQ_LEN]
    skip_grad = jnp.sum(cotangent.astype(jnp.float32) * feature.astype(jnp.float32), axis=(0, 2))
    return input_grad.astype(jnp.bfloat16), filter_grad, skip_grad
```

```python
import math

import jax
import jax.numpy as jnp
from jax import lax
from jax.experimental import pallas as pl
from jax.experimental.pallas import tpu as pltpu
from jax.sharding import PartitionSpec as P

def tables(n):
    p = jnp.arange(n, dtype=jnp.int32)
    def cis(num, den):
        ang = (num % den).astype(jnp.float32) * (2.0 * math.pi / den)
        return jnp.cos(ang), -jnp.sin(ang)
    quarter = 4 * p + 1
    o_re, o_im = cis(quarter[:, None] * p[None, :], 4 * n)
    t_re, t_im = cis(quarter[:, None] * p[None, :], 4 * n * n)
    i_re, i_im = cis(p[:, None] * p[None, :], n)
    bf = jnp.bfloat16
    fwd_outer = jnp.concatenate([o_re, o_im], 0).astype(bf)
    fwd_inner = jnp.concatenate([jnp.concatenate([i_re, i_im], 1), jnp.concatenate([-i_im, i_re], 1)], 0).astype(bf)
    inv_inner = jnp.concatenate([jnp.concatenate([i_re, -i_im], 1), jnp.concatenate([i_im, i_re], 1)], 0).astype(bf)
    inv_outer = (jnp.concatenate([o_re.T, o_im.T], 1) * (1.0 / (n * n))).astype(bf)
    return fwd_outer, t_re, t_im, fwd_inner, inv_inner, inv_outer

def core(x_ref, h_ref, taps_ref, fo_ref, tr_ref, ti_ref, fi_ref, ii_ref, io_ref, ig_ref, fg_ref, sk_ref,
         xs, hs, os, gs, bs, ys, zs, ds):
    n = 128; nb = 4; ch = 8
    f32, bf = jnp.float32, jnp.bfloat16
    def expand(k, _):
        xs[pl.ds(pl.multiple_of(k*256,256), 256), :] = x_ref[pl.ds(k*16,16)].astype(f32).reshape(256, n)
        return 0
    lax.fori_loop(0, 32, expand, 0)
    def expand_h(k, _):
        hs[pl.ds(pl.multiple_of(k*256,256), 256), :] = h_ref[pl.ds(k*16,16)].astype(f32).reshape(256, n)
        return 0
    lax.fori_loop(0, 4, expand_h, 0)
    lane = lax.broadcasted_iota(jnp.int32, (n, n), 1)
    row = lax.broadcasted_iota(jnp.int32, (n, n), 0)

    def shifted(v, m):
        here = pltpu.roll(v, n - m, 1)
        below = jnp.where(row == n - 1, 0.0, pltpu.roll(here, n - 1, 0))
        return jnp.where(lane >= n - m, below, here)

    def channel(c, _):
        sk = jnp.zeros((8, n), f32)
        for b in range(nb):
            feat = xs[pl.ds(b*16 + c, n, stride=64), :]
            cot = xs[pl.ds(b*16 + 8 + c, n, stride=64), :]
            ds[:, b*n:(b+1)*n] = feat.astype(bf)
            ds[:, (nb+b)*n:(nb+b+1)*n] = cot.astype(bf)
            sk = sk + jnp.sum((feat*cot).reshape(16, 8, n), axis=0)
        ds[:, 2*nb*n:] = hs[pl.ds(c, n, stride=8), :].astype(bf)
        sk_ref[pl.ds(c, 1), :] = jnp.sum(sk, axis=0, keepdims=True)
        first = jnp.dot(fo_ref[...], ds[...], preferred_element_type=f32)
        tr, ti = tr_ref[...], ti_ref[...]
        for s in range(2*nb+1):
            re = first[:n, s*n:(s+1)*n]; im = first[n:, s*n:(s+1)*n]
            bs[s*n:(s+1)*n, :n] = (re*tr - im*ti).astype(bf)
            bs[s*n:(s+1)*n, n:] = (re*ti + im*tr).astype(bf)
        spec = jnp.dot(bs[...], fi_ref[...], preferred_element_type=f32)
        h_re, h_im = spec[2*nb*n:, :n], spec[2*nb*n:, n:]
        g_re = jnp.zeros((n, n), f32); g_im = jnp.zeros((n, n), f32)
        for b in range(nb):
            f_re, f_im = spec[b*n:(b+1)*n, :n], spec[b*n:(b+1)*n, n:]
            c_re, c_im = spec[(nb+b)*n:(nb+b+1)*n, :n], spec[(nb+b)*n:(nb+b+1)*n, n:]
            ys[b*n:(b+1)*n, :n] = (h_re*c_re + h_im*c_im).astype(bf)
            ys[b*n:(b+1)*n, n:] = (h_re*c_im - h_im*c_re).astype(bf)
            g_re += f_re*c_re + f_im*c_im
            g_im += f_re*c_im - f_im*c_re
        ys[nb*n:, :n] = g_re.astype(bf)
        ys[nb*n:, n:] = g_im.astype(bf)
        back = jnp.dot(ys[...], ii_ref[...], preferred_element_type=f32)
        for s in range(nb+1):
            re = back[s*n:(s+1)*n, :n]; im = back[s*n:(s+1)*n, n:]
            zs[:n, s*n:(s+1)*n] = (re*tr + im*ti).astype(bf)
            zs[n:, s*n:(s+1)*n] = (im*tr - re*ti).astype(bf)
        out = jnp.dot(io_ref[...], zs[...], preferred_element_type=f32)
        gs[pl.ds(c, n, stride=8), :] = out[:, nb*n:]
        for b in range(nb):
            cot = xs[pl.ds(b*16 + 8 + c, n, stride=64), :]
            total = out[:, b*n:(b+1)*n] + taps_ref[c, 3]*cot
            res = taps_ref[c, 0]*total + taps_ref[c, 1]*shifted(total, 1) + taps_ref[c, 2]*shifted(total, 2)
            os[pl.ds(b*8 + c, n, stride=32), :] = res
        return 0
    lax.fori_loop(0, ch, channel, 0)
    def pack(k, _):
        ig_ref[pl.ds(k*16,16)] = os[pl.ds(pl.multiple_of(k*256,256), 256), :].reshape(16, 16, n).astype(bf)
        return 0
    lax.fori_loop(0, 16, pack, 0)
    def pack_g(k, _):
        fg_ref[pl.ds(k*16,16)] = gs[pl.ds(pl.multiple_of(k*256,256), 256), :].reshape(16, 16, n).astype(bf)
        return 0
    lax.fori_loop(0, 4, pack_g, 0)

def scratch():
    n=128
    return [pltpu.VMEM((8192,n),jnp.float32), pltpu.VMEM((1024,n),jnp.float32), pltpu.VMEM((4096,n),jnp.float32),
      pltpu.VMEM((1024,n),jnp.float32), pltpu.VMEM((9*n,2*n),jnp.bfloat16), pltpu.VMEM((5*n,2*n),jnp.bfloat16),
      pltpu.VMEM((2*n,5*n),jnp.bfloat16), pltpu.VMEM((n,9*n),jnp.bfloat16)]


def transform(x, h, taps):
    vm = pl.BlockSpec(memory_space=pltpu.VMEM)
    return pl.pallas_call(core,
      out_shape=(jax.ShapeDtypeStruct((256,16,128),jnp.bfloat16),jax.ShapeDtypeStruct((64,16,128),jnp.bfloat16),jax.ShapeDtypeStruct((8,128),jnp.float32)),
      in_specs=[vm,vm,pl.BlockSpec(memory_space=pltpu.SMEM)]+[vm]*6, out_specs=(vm,vm,vm),
      scratch_shapes=scratch(),
      compiler_params=pltpu.CompilerParams(vmem_limit_bytes=40<<20))(x,h,taps,*tables(128))


def body(feature, cotangent, long_filter, short_filter, skip_gain):
    rep = lax.axis_index("rep")
    owner = rep * 128 + lax.axis_index("grp") * 32 + lax.axis_index("seq")
    both = jnp.stack([feature[0].reshape(4, 128, 8, 128), cotangent[0].reshape(4, 128, 8, 128)], 2)
    both = both.transpose(1, 0, 2, 3, 4).reshape(512, 16, 128)
    x = lax.all_to_all(both, ("grp", "seq", "rep"), 0, 0, tiled=True)
    filt = lax.dynamic_slice_in_dim(long_filter, rep * 1024, 1024, 0).reshape(128, 8, 128)
    h = lax.all_to_all(filt, ("grp", "seq"), 0, 0, tiled=True).reshape(64, 16, 128)
    taps = jnp.concatenate([short_filter, skip_gain[:, None]], 1)
    taps = lax.dynamic_slice_in_dim(taps, owner * 8, 8, 0)
    ig, fg, sk = transform(x, h, taps)
    ig = lax.all_to_all(ig.reshape(512, 8, 128), ("grp", "seq", "rep"), 0, 0, tiled=True)
    ig = ig.reshape(128, 4, 8, 128).transpose(1, 0, 2, 3).reshape(1, 4096, 128)
    fg = lax.all_to_all(fg.reshape(128, 8, 128), ("grp", "seq"), 0, 0, tiled=True)
    fg = fg.reshape(1024, 128).astype(jnp.float32)
    sk = lax.all_gather(jnp.sum(sk, axis=1), ("rep", "grp", "seq"), tiled=True)
    return ig, fg, sk


def solution(mesh):
    return jax.shard_map(
        body,
        mesh=mesh,
        in_specs=(
            P("rep", None, ("grp", "seq")),
            P("rep", None, ("grp", "seq")),
            P(None, ("grp", "seq")),
            P(),
            P(),
        ),
        out_specs=(P("rep", None, ("grp", "seq")), P("rep", ("grp", "seq")), P()),
        check_vma=False,
    )
```

```python
import math

import jax
import jax.numpy as jnp
from jax import lax
from jax.experimental import pallas as pl
from jax.experimental.pallas import tpu as pltpu
from jax.sharding import PartitionSpec as P

MESH = pl.DeviceIdType.MESH
rem, div = lax.rem, lax.div
Z, V, R = 8, 16, 4
W = R * V
N = 128
F32, BF = jnp.float32, jnp.bfloat16
ZORDER = (4, 3, 5, 2, 6, 1, 7)
MIX = 27


def tables(n):
    p = jnp.arange(n, dtype=jnp.int32)
    def cis(num, den):
        ang = (num % den).astype(jnp.float32) * (2.0 * math.pi / den)
        return jnp.cos(ang), -jnp.sin(ang)
    quarter = 4 * p + 1
    o_re, o_im = cis(quarter[:, None] * p[None, :], 4 * n)
    t_re, t_im = cis(quarter[:, None] * p[None, :], 4 * n * n)
    i_re, i_im = cis(p[:, None] * p[None, :], n)
    bf = jnp.bfloat16
    fwd_outer = jnp.concatenate([o_re, o_im], 0).astype(bf)
    fwd_inner = jnp.concatenate([jnp.concatenate([i_re, i_im], 1), jnp.concatenate([-i_im, i_re], 1)], 0).astype(bf)
    inv_inner = jnp.concatenate([jnp.concatenate([i_re, -i_im], 1), jnp.concatenate([i_im, i_re], 1)], 0).astype(bf)
    inv_outer = (jnp.concatenate([o_re.T, o_im.T], 1) * (1.0 / (n * n))).astype(bf)
    return fwd_outer, t_re, t_im, fwd_inner, inv_inner, inv_outer


def place():
    g = lax.axis_index("grp")
    s = lax.axis_index("seq")
    r = lax.axis_index("rep")
    return g, div(r, 2) * 4 + div(s, Z), rem(s, Z), rem(r, 2)


def plane_id(x, y, core):
    return (div(y, 4) * 2 + core) * V + x * 4 + rem(y, 4)


def z_mate(k, me):
    to = rem(me[2] + k, Z)
    return to, {"seq": rem(me[1], 4) * Z + to}


def plane_device(x, y, core, me):
    return {"grp": x, "seq": rem(y, 4) * Z + me[2], "rep": div(y, 4) * 2 + core}


def w_mate(k, me):
    x = rem(me[0] + rem(k, 4), 4)
    core = rem(me[3] + rem(div(k, 4), 2), 2)
    y = rem(me[1] + div(k, 8), 8)
    return plane_id(x, y, core), plane_device(x, y, core, me)


def core_mate(k, core, me):
    x = rem(me[0] + rem(k, 4), 4)
    y = rem(me[1] + div(k, 4), 8)
    return div(y, 4) * V + x * 4 + rem(y, 4), plane_device(x, y, core, me)


def v_mate(k, me):
    x = rem(me[0] + rem(k, 4), 4)
    low = rem(rem(me[1], 4) + div(k, 4), 4)
    return x * 4 + low, {"grp": x, "seq": low * Z + me[2]}


def each(lo, hi, f):
    def step(k, carry):
        f(k)
        return carry

    lax.fori_loop(lo, hi, step, 0)


def greet(me):
    barrier = pltpu.get_barrier_semaphore()

    def signal(device):
        pl.semaphore_signal(barrier, inc=1, device_id=device, device_id_type=MESH)

    each(1, Z, lambda k: signal(z_mate(k, me)[1]))
    each(1, W, lambda k: signal(w_mate(k, me)[1]))
    pl.semaphore_wait(barrier, Z + W - 2)


def done(ref, sem):
    pltpu.make_async_copy(ref, ref, sem).wait()


def gather_inputs(me, f_ref, c_ref, h_ref, fx, cx, hx, ia, ib, ih, send, recv, loc):
    z = me[2]
    w = plane_id(me[0], me[1], me[3])
    r, v = div(w, V), rem(w, V)

    def remote(src, dst, i, device):
        pltpu.make_async_remote_copy(
            src, dst, send.at[i], recv.at[i], device_id=device, device_id_type=MESH
        ).start()

    def local(src, dst, i):
        copy = pltpu.make_async_copy(src, dst, loc.at[i])
        copy.start()
        return copy

    own = [
        local(f_ref.at[:, z], ia.at[z], 0),
        local(c_ref.at[r, :, v], ib.at[w], 1),
        local(h_ref.at[r, z], ih.at[z], 2),
    ]

    def cot_plane(k):
        to, device = w_mate(rem(k * MIX, W), me)
        remote(c_ref.at[div(to, V), :, rem(to, V)], ib.at[w], 1, device)

    for k in ZORDER:
        to, device = z_mate(k, me)
        remote(f_ref.at[:, to], ia.at[z], 0, device)
        remote(h_ref.at[r, to], ih.at[z], 4, device)
    each(1, W, cot_plane)
    for copy in own:
        copy.wait()
    done(ih.at[pl.ds(0, Z - 1)], recv.at[4])
    own_h = local(ih.at[:, v], hx.at[v], 0)

    def filt_plane(k):
        to, device = v_mate(k, me)
        remote(ih.at[:, to], hx.at[v], 5, device)

    each(1, V, filt_plane)
    done(ia.at[pl.ds(0, Z - 1)], recv.at[0])
    own_f = local(ia.at[:, r, v], fx.at[w], 1)

    def feat_plane(k):
        to, device = w_mate(rem(k * MIX, W), me)
        remote(ia.at[:, div(to, V), rem(to, V)], fx.at[w], 2, device)

    each(1, W, feat_plane)
    done(ib.at[pl.ds(0, W - 1)], recv.at[1])
    own_c = local(ib.at[:, z], cx.at[:, z], 2)
    for k in ZORDER:
        to, device = z_mate(k, me)
        remote(ib.at[:, to], cx.at[:, z], 3, device)
    own_h.wait()
    own_f.wait()
    own_c.wait()
    for i in (0, 1, 2, 3):
        done(fx.at[pl.ds(0, W - 1)] if i in (1, 2) else cx.at[:, pl.ds(0, Z - 1)], send.at[i])
    done(ih.at[pl.ds(0, Z - 1)], send.at[4])
    done(hx.at[pl.ds(0, V - 1)], send.at[5])
    done(hx.at[pl.ds(0, V - 1)], recv.at[5])
    done(fx.at[pl.ds(0, W - 1)], recv.at[2])
    done(cx.at[:, pl.ds(0, Z - 1)], recv.at[3])


def shifted(values, m):
    lane = lax.broadcasted_iota(jnp.int32, (N, N), 1)
    row = lax.broadcasted_iota(jnp.int32, (N, N), 0)
    here = pltpu.roll(values, N - m, 1)
    below = jnp.where(row == N - 1, 0.0, pltpu.roll(here, N - 1, 0))
    return jnp.where(lane >= N - m, below, here)


def transform(me, fx, cx, hx, taps_ref, tabs, oa, ob, go, sk, fs, cs, hs, os, gs, ds, bs, ys, zs):
    fo_ref, tr_ref, ti_ref, fi_ref, ii_ref, io_ref = tabs
    rows = Z * 8

    def expand(w):
        at = pl.ds(pl.multiple_of(w * rows, rows), rows)
        fs[at, :] = fx[w].astype(F32).reshape(rows, N)
        cs[at, :] = cx[w].astype(F32).reshape(rows, N)

    each(0, W, expand)

    def expand_h(v):
        hs[pl.ds(pl.multiple_of(v * rows, rows), rows), :] = hx[v].astype(F32).reshape(rows, N)

    each(0, V, expand_h)
    sk[...] = jnp.zeros((1, N), F32)
    sig_c, sig_h = R, 2 * R

    def channel(c):
        total = jnp.zeros((8, N), F32)
        for b in range(R):
            feat = fs[pl.ds(b * 8 * N + c, N, stride=8), :]
            cot = cs[pl.ds(b * 8 * N + c, N, stride=8), :]
            ds[:, b * N:(b + 1) * N] = feat.astype(BF)
            ds[:, (sig_c + b) * N:(sig_c + b + 1) * N] = cot.astype(BF)
            total = total + jnp.sum((feat * cot).reshape(N // 8, 8, N), axis=0)
        ds[:, sig_h * N:] = hs[pl.ds(c, N, stride=8), :].astype(BF)
        total = jnp.sum(jnp.sum(total, axis=0, keepdims=True), axis=1, keepdims=True)
        lane = lax.broadcasted_iota(jnp.int32, (1, N), 1)
        sk[...] += jnp.where(lane == me[2] * 8 + c, total, 0.0)
        first = jnp.dot(fo_ref[...], ds[...], preferred_element_type=F32)
        tr, ti = tr_ref[...], ti_ref[...]
        for s in range(2 * R + 1):
            re, im = first[:N, s * N:(s + 1) * N], first[N:, s * N:(s + 1) * N]
            bs[s * N:(s + 1) * N, :N] = (re * tr - im * ti).astype(BF)
            bs[s * N:(s + 1) * N, N:] = (re * ti + im * tr).astype(BF)
        spec = jnp.dot(bs[...], fi_ref[...], preferred_element_type=F32)

        def part(s):
            return spec[s * N:(s + 1) * N, :N], spec[s * N:(s + 1) * N, N:]

        h_re, h_im = part(sig_h)
        g_re = jnp.zeros((N, N), F32)
        g_im = jnp.zeros((N, N), F32)
        for b in range(R):
            f_re, f_im = part(b)
            c_re, c_im = part(sig_c + b)
            ys[b * N:(b + 1) * N, :N] = (h_re * c_re + h_im * c_im).astype(BF)
            ys[b * N:(b + 1) * N, N:] = (h_re * c_im - h_im * c_re).astype(BF)
            g_re += f_re * c_re + f_im * c_im
            g_im += f_re * c_im - f_im * c_re
        ys[R * N:, :N] = g_re.astype(BF)
        ys[R * N:, N:] = g_im.astype(BF)
        back = jnp.dot(ys[...], ii_ref[...], preferred_element_type=F32)
        for s in range(R + 1):
            re, im = back[s * N:(s + 1) * N, :N], back[s * N:(s + 1) * N, N:]
            zs[:N, s * N:(s + 1) * N] = (re * tr + im * ti).astype(BF)
            zs[N:, s * N:(s + 1) * N] = (im * tr - re * ti).astype(BF)
        out = jnp.dot(io_ref[...], zs[...], preferred_element_type=F32)
        gs[pl.ds(c, N, stride=8), :] = out[:, R * N:]
        for b in range(R):
            cot = cs[pl.ds(b * 8 * N + c, N, stride=8), :]
            grad = out[:, b * N:(b + 1) * N] + taps_ref[c, 3] * cot
            res = (
                taps_ref[c, 0] * grad
                + taps_ref[c, 1] * shifted(grad, 1)
                + taps_ref[c, 2] * shifted(grad, 2)
            )
            os[pl.ds(b * 8 * N + c, N, stride=8), :] = res

    each(0, 8, channel)

    def pack(q):
        half, v = div(q, V), rem(q, V)
        base = (half * 2) * 8 * N + v * rows
        for z in range(Z):
            oa[z, q] = os[pl.ds(pl.multiple_of(base + z * 8, 8), 8), :].astype(BF)
        base = base + 8 * N
        ob[q] = os[pl.ds(pl.multiple_of(base, rows), rows), :].reshape(Z, 8, N).astype(BF)

    each(0, W // 2, pack)

    def pack_g(v):
        for z in range(Z):
            go[z, v] = gs[pl.ds(pl.multiple_of(v * rows + z * 8, 8), 8), :].astype(BF)

    each(0, V, pack_g)


def scatter_outputs(me, oa, ob, go, sk, out, out_g, out_s, ia, ib, tally, ig, si, mid, send, recv, loc):
    z, core = me[2], me[3]
    w = plane_id(me[0], me[1], core)
    r, v = div(w, V), rem(w, V)
    q = div(r, 2) * V + v

    def remote(src, dst, i, device):
        pltpu.make_async_remote_copy(
            src, dst, send.at[i], recv.at[i], device_id=device, device_id_type=MESH
        ).start()

    def local(src, dst, i):
        copy = pltpu.make_async_copy(src, dst, loc.at[i])
        copy.start()
        return copy

    def one_plane(k):
        to, device = core_mate(rem(k * MIX, W // 2), 1, me)
        remote(ob.at[to], ib.at[r, v], 8, device)

    own = [local(oa.at[z], ia.at[z], 0), local(go.at[z], ig.at[z], 1), local(sk, si.at[z], 2)]
    for k in ZORDER:
        to, device = z_mate(k, me)
        remote(oa.at[to], ia.at[z], 6, device)
        remote(go.at[to], ig.at[z], 10, device)
        remote(sk, si.at[z], 12, device)
    each(core, W // 2, one_plane)
    for copy in own:
        copy.wait()

    @pl.when(core == 1)
    def _():
        local(ob.at[q], ib.at[r, v], 0).wait()

    done(si.at[pl.ds(0, Z - 1)], recv.at[12])
    mid[...] = jnp.sum(si[...], axis=0)
    own_s = local(mid, out_s.at[w], 2)

    def sums_plane(k):
        to, device = w_mate(rem(k * MIX, W), me)
        remote(mid, out_s.at[w], 13, device)

    each(1, W, sums_plane)
    done(ia.at[pl.ds(0, Z - 1)], recv.at[6])

    @pl.when(core == 0)
    def _():
        local(ia.at[:, q], out.at[r, :, v], 0).wait()

    def zero_plane(k):
        to, device = core_mate(rem(k * MIX, W // 2), 0, me)
        remote(ia.at[:, to], out.at[r, :, v], 7, device)

    each(1 - core, W // 2, zero_plane)
    done(ig.at[pl.ds(0, Z - 1)], recv.at[10])
    own_g = local(ig.at[:, v], out_g.at[:, v], 1)

    def grad_plane(k):
        to, device = v_mate(k, me)
        remote(ig.at[:, to], out_g.at[:, v], 11, device)

    each(1, V, grad_plane)

    @pl.when(core == 1)
    def _():
        done(tally.at[pl.ds(0, W - 1)], recv.at[8])
        own_b = local(ib.at[:, :, z], out.at[:, z], 0)
        for k in ZORDER:
            to, device = z_mate(k, me)
            remote(ib.at[:, :, to], out.at[:, z], 9, device)
        own_b.wait()
        done(tally.at[:, pl.ds(0, Z - 1)], send.at[9])
        done(tally.at[pl.ds(0, W // 2 - 1)], send.at[8])
        done(tally.at[pl.ds(0, W // 2)], send.at[7])
        done(tally.at[:, pl.ds(0, Z - 1)], recv.at[9])

    @pl.when(core == 0)
    def _():
        done(tally.at[pl.ds(0, W // 2)], send.at[8])
        done(tally.at[pl.ds(0, W // 2 - 1)], send.at[7])
        done(tally.at[pl.ds(0, W - 1)], recv.at[7])

    own_s.wait()
    own_g.wait()
    done(ia.at[pl.ds(0, Z - 1)], send.at[6])
    done(ig.at[pl.ds(0, Z - 1)], send.at[10])
    done(out_g.at[:, pl.ds(0, V - 1)], send.at[11])
    done(out_g.at[:, pl.ds(0, V - 1)], recv.at[11])
    done(si.at[pl.ds(0, Z - 1)], send.at[12])
    done(out_s.at[pl.ds(0, W - 1)], send.at[13])
    done(out_s.at[pl.ds(0, W - 1)], recv.at[13])


def kernel(
    f_ref, c_ref, h_ref, taps_ref, fo_ref, tr_ref, ti_ref, fi_ref, ii_ref, io_ref,
    out, out_g, out_s,
    ia, ib, ih, fx, cx, hx, fs, cs, hs, os, gs, ds, bs, ys, zs,
    oa, ob, go, sk, ia2, ib2, ig2, si, mid, send, recv, loc,
):
    me = place()
    greet(me)
    gather_inputs(me, f_ref, c_ref, h_ref, fx, cx, hx, ia, ib, ih, send, recv, loc)
    tabs = (fo_ref, tr_ref, ti_ref, fi_ref, ii_ref, io_ref)
    transform(me, fx, cx, hx, taps_ref, tabs, oa, ob, go, sk, fs, cs, hs, os, gs, ds, bs, ys, zs)
    scatter_outputs(me, oa, ob, go, sk, out, out_g, out_s, ia2, ib2, fx, ig2, si, mid, send, recv, loc)


def run(feature, cotangent, long_filter, taps):
    def bf(*shape):
        return pltpu.VMEM(shape + (8, N), BF)

    def f32(*shape):
        return pltpu.VMEM(shape, F32)

    vm = pl.BlockSpec(memory_space=pltpu.VMEM)
    whole = pl.BlockSpec(memory_space=pl.ANY)
    return pl.pallas_call(
        kernel,
        out_shape=(
            jax.ShapeDtypeStruct((R, Z, V, 8, N), BF),
            jax.ShapeDtypeStruct((Z, V, 8, N), BF),
            jax.ShapeDtypeStruct((W, 1, N), F32),
        ),
        in_specs=[whole] * 3 + [pl.BlockSpec(memory_space=pltpu.SMEM)] + [vm] * 6,
        out_specs=(vm, vm, vm),
        scratch_shapes=[
            bf(Z, R, V), bf(W, Z), bf(Z, V), bf(W, Z), bf(W, Z), bf(V, Z),
            f32(W * Z * 8, N), f32(W * Z * 8, N), f32(V * Z * 8, N), f32(W * Z * 8, N), f32(V * Z * 8, N),
            pltpu.VMEM((N, 9 * N), BF), pltpu.VMEM((9 * N, 2 * N), BF),
            pltpu.VMEM((5 * N, 2 * N), BF), pltpu.VMEM((2 * N, 5 * N), BF),
            bf(Z, W // 2), bf(W // 2, Z), bf(Z, V), f32(1, N),
            bf(Z, W // 2), bf(R, V, Z), bf(Z, V), f32(Z, 1, N), f32(1, N),
            pltpu.SemaphoreType.DMA((14,)), pltpu.SemaphoreType.DMA((14,)), pltpu.SemaphoreType.DMA((3,)),
        ],
        compiler_params=pltpu.CompilerParams(
            collective_id=0, has_side_effects=True, vmem_limit_bytes=48 << 20
        ),
    )(feature, cotangent, long_filter, taps, *tables(N))


def body(feature, cotangent, long_filter, short_filter, skip_gain):
    rep, grp, seq = lax.axis_index("rep"), lax.axis_index("grp"), lax.axis_index("seq")
    first = rep * 1024 + seq % Z * 128 + (grp * 4 + seq // Z) * 8
    taps = jnp.concatenate([short_filter, skip_gain[:, None]], 1)
    taps = lax.dynamic_slice_in_dim(taps, first, 8, 0)
    shape = (R, Z, V, 8, N)
    grad, filt, sums = run(
        feature.reshape(shape), cotangent.reshape(shape), long_filter.reshape(shape), taps
    )
    sums = sums[:, 0, :Z * 8].reshape(R, V, Z, 8).transpose(0, 2, 1, 3).reshape(-1)
    return grad.reshape(1, -1, N), filt.reshape(-1, N).astype(F32), sums


def solution(mesh):
    return jax.shard_map(
        body,
        mesh=mesh,
        in_specs=(
            P("rep", None, ("grp", "seq")),
            P("rep", None, ("grp", "seq")),
            P(None, ("grp", "seq")),
            P(),
            P(),
        ),
        out_specs=(P("rep", None, ("grp", "seq")), P("rep", ("grp", "seq")), P()),
        check_vma=False,
    )
```

```python
import math

import jax
import jax.numpy as jnp
import ml_dtypes
import numpy as np
from jax import lax
from jax.experimental import pallas as pl
from jax.experimental.pallas import tpu as pltpu
from jax.sharding import PartitionSpec as P

MESH = pl.DeviceIdType.MESH
rem, div = lax.rem, lax.div
Z, V, R = 8, 16, 4
W = R * V
N = 128
F32, BF = jnp.float32, jnp.bfloat16
ZORDER = (4, 3, 5, 2, 6, 1, 7)
MIX = 27
LIMIT = 60
H1, H2, C0, F0, G1, G2, O0, S1, S2, S3 = 0, 1, 2, 6, 10, 11, 12, 16, 17, 18


def tables(n):
    p = np.arange(n)

    def cis(num, den):
        angle = (num % den) * (2.0 * math.pi / den)
        return np.cos(angle), -np.sin(angle)

    quarter = 4 * p + 1
    o_re, o_im = cis(quarter[:, None] * p[None, :], 4 * n)
    t_re, t_im = cis(quarter[:, None] * p[None, :], 4 * n * n)
    i_re, i_im = cis(p[:, None] * p[None, :], n)
    fwd_outer = np.concatenate([o_re, o_im], 0)
    fwd_inner = np.block([[i_re, i_im], [-i_im, i_re]])
    inv_inner = np.block([[i_re, -i_im], [i_im, i_re]])
    inv_outer = np.concatenate([o_re.T, o_im.T], 1) / (n * n)
    half = ml_dtypes.bfloat16
    return (
        fwd_outer.astype(half), t_re.astype(np.float32), t_im.astype(np.float32),
        fwd_inner.astype(half), inv_inner.astype(half), inv_outer.astype(half),
    )


def place():
    g = lax.axis_index("grp")
    s = lax.axis_index("seq")
    r = lax.axis_index("rep")
    return g, div(r, 2) * 4 + div(s, Z), rem(s, Z), rem(r, 2)


def z_mate(k, me):
    to = rem(me[2] + k, Z)
    return to, {"seq": rem(me[1], 4) * Z + to}


def plane_device(x, y, core, me):
    return {"grp": x, "seq": rem(y, 4) * Z + me[2], "rep": div(y, 4) * 2 + core}


def core_mate(k, core, me):
    x = rem(me[0] + rem(k, 4), 4)
    y = rem(me[1] + div(k, 4), 8)
    return div(y, 4), x * 4 + rem(y, 4), plane_device(x, y, core, me)


def v_mate(k, me):
    x = rem(me[0] + rem(k, 4), 4)
    low = rem(rem(me[1], 4) + div(k, 4), 4)
    return x * 4 + low, {"grp": x, "seq": low * Z + me[2]}


def each(lo, hi, f):
    def step(k, carry):
        f(k)
        return carry

    lax.fori_loop(lo, hi, step, 0)


def y_device(k, me):
    y = rem(me[1] + k, 8)
    return {"seq": rem(y, 4) * Z + me[2], "rep": div(y, 4) * 2 + me[3]}


def xc_device(k, me):
    return {"grp": rem(me[0] + rem(k, 4), 4), "rep": div(me[1], 4) * 2 + rem(me[3] + div(k, 4), 2)}


def r_mate(k, me):
    r = rem(div(me[1], 4) * 2 + me[3] + k, R)
    return r, {"rep": r}


def signal(sem, device):
    pl.semaphore_signal(sem, inc=1, device_id=device, device_id_type=MESH)


def greet(me, gate):
    barrier = pltpu.get_barrier_semaphore()
    each(1, Z, lambda k: signal(barrier, z_mate(k, me)[1]))
    each(1, 8, lambda k: signal(barrier, xc_device(k, me)))
    each(1, 8, lambda k: signal(barrier, y_device(k, me)))
    pl.semaphore_wait(barrier, 21)
    each(1, 8, lambda k: signal(gate, xc_device(k, me)))


def done(ref, sem):
    pltpu.make_async_copy(ref, ref, sem).wait()


class Links:
    def __init__(self, me, send, recv, loc):
        self.me, self.send, self.recv, self.loc = me, send, recv, loc
        self.z, self.core = me[2], me[3]
        self.v = me[0] * 4 + rem(me[1], 4)
        self.high = div(me[1], 4)
        self.r = self.high * 2 + self.core

    def remote(self, src, dst, i, device):
        pltpu.make_async_remote_copy(
            src, dst, self.send.at[i], self.recv.at[i], device_id=device, device_id_type=MESH
        ).start()

    def local(self, src, dst, i):
        copy = pltpu.make_async_copy(src, dst, self.loc.at[i])
        copy.start()
        return copy


def shifted(values, m):
    lane = lax.broadcasted_iota(jnp.int32, (N, N), 1)
    row = lax.broadcasted_iota(jnp.int32, (N, N), 0)
    here = pltpu.roll(values, N - m, 1)
    below = jnp.where(row == N - 1, 0.0, pltpu.roll(here, N - 1, 0))
    return jnp.where(lane >= N - m, below, here)


class Exchange:
    def __init__(self, links, base, for_zero, for_one, ia, ib, dst, tally):
        self.ln, self.base = links, base
        self.for_zero, self.for_one = for_zero, for_one
        self.ia, self.ib, self.dst, self.tally = ia, ib, dst, tally

    def first_z(self):
        ln = self.ln
        for k in ZORDER:
            to, device = z_mate(k, ln.me)
            ln.remote(self.for_zero(to), self.ia.at[ln.z], self.base, device)

    def first_plane(self):
        ln = self.ln

        def one(k):
            high, v, device = core_mate(rem(k * MIX, W // 2), 1, ln.me)
            ln.remote(self.for_one(high, v), self.ib.at[ln.r, ln.v], self.base + 2, device)

        each(ln.core, W // 2, one)

    def own_first(self):
        ln = self.ln
        ln.local(self.for_zero(ln.z), self.ia.at[ln.z], 0).wait()

        @pl.when(ln.core == 1)
        def _():
            ln.local(self.for_one(ln.high, ln.v), self.ib.at[ln.r, ln.v], 1).wait()

    def second(self):
        ln = self.ln
        done(self.ia.at[pl.ds(0, Z - 1)], ln.recv.at[self.base])

        def one(k):
            high, v, device = core_mate(rem(k * MIX, W // 2), 0, ln.me)
            ln.remote(self.ia.at[:, high, v], self.dst.at[ln.r, :, ln.v], self.base + 1, device)

        each(1 - ln.core, W // 2, one)

        @pl.when(ln.core == 0)
        def _():
            ln.local(self.ia.at[:, ln.high, ln.v], self.dst.at[ln.r, :, ln.v], 0).wait()

        @pl.when(ln.core == 1)
        def _():
            done(self.tally.at[pl.ds(0, W - 1)], ln.recv.at[self.base + 2])
            for k in ZORDER:
                to, device = z_mate(k, ln.me)
                ln.remote(self.ib.at[:, :, to], self.dst.at[:, ln.z], self.base + 3, device)
            ln.local(self.ib.at[:, :, ln.z], self.dst.at[:, ln.z], 1).wait()

    def arrived(self):
        ln = self.ln

        @pl.when(ln.core == 0)
        def _():
            done(self.tally.at[pl.ds(0, W - 1)], ln.recv.at[self.base + 1])

        @pl.when(ln.core == 1)
        def _():
            done(self.tally.at[:, pl.ds(0, Z - 1)], ln.recv.at[self.base + 3])

    def sent(self):
        ln = self.ln
        done(self.ia.at[pl.ds(0, Z - 1)], ln.send.at[self.base])

        @pl.when(ln.core == 0)
        def _():
            done(self.tally.at[pl.ds(0, W // 2)], ln.send.at[self.base + 2])
            done(self.tally.at[pl.ds(0, W // 2 - 1)], ln.send.at[self.base + 1])

        @pl.when(ln.core == 1)
        def _():
            done(self.tally.at[pl.ds(0, W // 2 - 1)], ln.send.at[self.base + 2])
            done(self.tally.at[pl.ds(0, W // 2)], ln.send.at[self.base + 1])
            done(self.tally.at[:, pl.ds(0, Z - 1)], ln.send.at[self.base + 3])


class SmallExchange:
    def __init__(self, links, base, src, ih, dst):
        self.ln, self.base, self.src, self.ih, self.dst = links, base, src, ih, dst

    def first(self):
        ln = self.ln
        for k in ZORDER:
            to, device = z_mate(k, ln.me)
            ln.remote(self.src(to), self.ih.at[ln.z], self.base, device)

    def own_first(self):
        self.ln.local(self.src(self.ln.z), self.ih.at[self.ln.z], 2).wait()

    def second(self):
        ln = self.ln
        done(self.ih.at[pl.ds(0, Z - 1)], ln.recv.at[self.base])

        def one(k):
            to, device = v_mate(k, ln.me)
            ln.remote(self.ih.at[:, to], self.dst.at[:, ln.v], self.base + 1, device)

        each(1, V, one)
        ln.local(self.ih.at[:, ln.v], self.dst.at[:, ln.v], 2).wait()

    def arrived(self):
        done(self.dst.at[:, pl.ds(0, V - 1)], self.ln.recv.at[self.base + 1])

    def sent(self):
        done(self.ih.at[pl.ds(0, Z - 1)], self.ln.send.at[self.base])
        done(self.dst.at[:, pl.ds(0, V - 1)], self.ln.send.at[self.base + 1])


class Sums:
    def __init__(self, links, sk, sv, mid, si, dst):
        self.ln, self.sk, self.sv, self.mid, self.si, self.dst = links, sk, sv, mid, si, dst

    def first(self):
        ln = self.ln

        def one(k):
            ln.remote(self.sk, self.sv.at[ln.v], S1, v_mate(k, ln.me)[1])

        each(1, V, one)
        ln.local(self.sk, self.sv.at[ln.v], 0).wait()

    def second(self):
        ln = self.ln
        done(self.sv.at[pl.ds(0, V - 1)], ln.recv.at[S1])
        self.mid[...] = jnp.sum(self.sv[...], axis=0)
        for k in ZORDER:
            ln.remote(self.mid, self.si.at[ln.z], S2, z_mate(k, ln.me)[1])
        ln.local(self.mid, self.si.at[ln.z], 0).wait()

    def third(self):
        ln = self.ln
        done(self.si.at[pl.ds(0, Z - 1)], ln.recv.at[S2])
        for k in range(1, R):
            ln.remote(self.si, self.dst.at[ln.r], S3, r_mate(k, ln.me)[1])
        ln.local(self.si, self.dst.at[ln.r], 0).wait()

    def finish(self):
        ln = self.ln
        done(self.sv.at[pl.ds(0, V - 1)], ln.send.at[S1])
        done(self.si.at[pl.ds(0, Z - 1)], ln.send.at[S2])
        done(self.dst.at[pl.ds(0, R - 1)], ln.send.at[S3])
        done(self.dst.at[pl.ds(0, R - 1)], ln.recv.at[S3])


def spread(dst, src):
    def one(q):
        r, v = div(q, V), rem(q, V)
        for z in range(Z):
            at = pl.multiple_of(r * 8 * N + v * Z * 8 + z * 8, 8)
            dst[pl.ds(at, 8), :] = src[r, z, v].astype(F32)

    each(0, W, one)


def twisted(bs, first, tr, ti, count):
    for s in range(count):
        re, im = first[:N, s * N:(s + 1) * N], first[N:, s * N:(s + 1) * N]
        bs[s * N:(s + 1) * N, :N] = (re * tr - im * ti).astype(BF)
        bs[s * N:(s + 1) * N, N:] = (re * ti + im * tr).astype(BF)


def untwisted(zs, back, tr, ti, count):
    for s in range(count):
        re, im = back[s * N:(s + 1) * N, :N], back[s * N:(s + 1) * N, N:]
        zs[:N, s * N:(s + 1) * N] = (re * tr + im * ti).astype(BF)
        zs[N:, s * N:(s + 1) * N] = (im * tr - re * ti).astype(BF)


def input_part(cx, hx, taps_ref, tabs, oa, ob, spec_c, cs, hs, os, ds, bs, ys, zs):
    fo_ref, tr_ref, ti_ref, fi_ref, ii_ref, io_ref = tabs
    spread(cs, cx)

    def expand_h(v):
        for z in range(Z):
            hs[pl.ds(pl.multiple_of(v * Z * 8 + z * 8, 8), 8), :] = hx[z, v].astype(F32)

    each(0, V, expand_h)

    def channel(c):
        for b in range(R):
            ds[:, b * N:(b + 1) * N] = cs[pl.ds(b * 8 * N + c, N, stride=8), :].astype(BF)
        ds[:, R * N:] = hs[pl.ds(c, N, stride=8), :].astype(BF)
        tr, ti = tr_ref[...], ti_ref[...]
        first = jnp.dot(fo_ref[...], ds[...], preferred_element_type=F32)
        twisted(bs, first, tr, ti, R + 1)
        spec = jnp.dot(bs[...], fi_ref[...], preferred_element_type=F32)
        spec_c[c] = spec[:R * N]
        h_re, h_im = spec[R * N:, :N], spec[R * N:, N:]
        for b in range(R):
            c_re, c_im = spec[b * N:(b + 1) * N, :N], spec[b * N:(b + 1) * N, N:]
            ys[b * N:(b + 1) * N, :N] = (h_re * c_re + h_im * c_im).astype(BF)
            ys[b * N:(b + 1) * N, N:] = (h_re * c_im - h_im * c_re).astype(BF)
        back = jnp.dot(ys[...], ii_ref[...], preferred_element_type=F32)
        untwisted(zs, back, tr, ti, R)
        out = jnp.dot(io_ref[...], zs[...], preferred_element_type=F32)
        for b in range(R):
            cot = cs[pl.ds(b * 8 * N + c, N, stride=8), :]
            grad = out[:, b * N:(b + 1) * N] + taps_ref[c, 3] * cot
            res = (
                taps_ref[c, 0] * grad
                + taps_ref[c, 1] * shifted(grad, 1)
                + taps_ref[c, 2] * shifted(grad, 2)
            )
            os[pl.ds(b * 8 * N + c, N, stride=8), :] = res

    each(0, 8, channel)

    def pack(q):
        high, v = div(q, V), rem(q, V)
        base = high * 16 * N + v * Z * 8
        for z in range(Z):
            oa[z, high, v] = os[pl.ds(pl.multiple_of(base + z * 8, 8), 8), :].astype(BF)
        base = base + 8 * N
        ob[high, v] = os[pl.ds(pl.multiple_of(base, 64), 64), :].reshape(Z, 8, N).astype(BF)

    each(0, W // 2, pack)


def sums_part(links, fx, cs, fs, sk):
    def one(q, total):
        r, v = div(q, V), rem(q, V)
        for z in range(Z):
            at = pl.ds(pl.multiple_of(r * 8 * N + v * Z * 8 + z * 8, 8), 8)
            feat = fx[r, z, v].astype(F32)
            fs[at, :] = feat
            total = total + feat * cs[at, :]
        return total

    total = lax.fori_loop(0, W, one, jnp.zeros((8, N), F32))
    total = jnp.sum(total, axis=1, keepdims=True)
    lane = lax.broadcasted_iota(jnp.int32, (8, N), 1)
    spot = lax.broadcasted_iota(jnp.int32, (8, N), 0) + links.v * 8
    sk[...] = jnp.sum(jnp.where(lane == spot, total, 0.0), axis=0, keepdims=True)


def filter_part(tabs, go, spec_c, fs, gs, ds, bs, ys, zs):
    fo_ref, tr_ref, ti_ref, fi_ref, ii_ref, io_ref = tabs

    def channel(c):
        for b in range(R):
            ds[:, b * N:(b + 1) * N] = fs[pl.ds(b * 8 * N + c, N, stride=8), :].astype(BF)
        tr, ti = tr_ref[...], ti_ref[...]
        first = jnp.dot(fo_ref[...], ds[:, :R * N], preferred_element_type=F32)
        twisted(bs, first, tr, ti, R)
        spec = jnp.dot(bs[:R * N, :], fi_ref[...], preferred_element_type=F32)
        g_re = jnp.zeros((N, N), F32)
        g_im = jnp.zeros((N, N), F32)
        for b in range(R):
            f_re, f_im = spec[b * N:(b + 1) * N, :N], spec[b * N:(b + 1) * N, N:]
            c_re = spec_c[c, b * N:(b + 1) * N, :N]
            c_im = spec_c[c, b * N:(b + 1) * N, N:]
            g_re += f_re * c_re + f_im * c_im
            g_im += f_re * c_im - f_im * c_re
        ys[:N, :N] = g_re.astype(BF)
        ys[:N, N:] = g_im.astype(BF)
        back = jnp.dot(ys[:N, :], ii_ref[...], preferred_element_type=F32)
        untwisted(zs, back, tr, ti, 1)
        out = jnp.dot(io_ref[...], zs[:, :N], preferred_element_type=F32)
        gs[pl.ds(c, N, stride=8), :] = out

    each(0, 8, channel)

    def pack(v):
        for z in range(Z):
            go[z, v] = gs[pl.ds(pl.multiple_of(v * Z * 8 + z * 8, 8), 8), :].astype(BF)

    each(0, V, pack)


def kernel(
    f_ref, c_ref, h_ref, taps_ref, fo_ref, tr_ref, ti_ref, fi_ref, ii_ref, io_ref,
    out, out_g, out_s,
    ic, jc, if_, jf, io, jo, ih, ig, cx, fx, hx, oa, ob, go, tally,
    spec_c, cs, fs, hs, os, gs, ds, bs, ys, zs,
    sk, sv, mid, si, gate, send, recv, loc,
):
    me = place()
    tabs = (fo_ref, tr_ref, ti_ref, fi_ref, ii_ref, io_ref)
    ln = Links(me, send, recv, loc)
    filt = SmallExchange(ln, H1, lambda z: h_ref.at[ln.r, z], ih, hx)
    cot = Exchange(
        ln, C0, lambda z: c_ref.at[:, 0, z], lambda y, v: c_ref.at[y, 1, :, v], ic, jc, cx, tally
    )
    feat = Exchange(
        ln, F0, lambda z: f_ref.at[:, 0, z], lambda y, v: f_ref.at[y, 1, :, v], if_, jf, fx, tally
    )
    grad = Exchange(ln, O0, lambda z: oa.at[z], lambda y, v: ob.at[y, v], io, jo, out, tally)
    fgrad = SmallExchange(ln, G1, lambda z: go.at[z], ig, out_g)
    sums = Sums(ln, sk, sv, mid, si, out_s)

    greet(me, gate)
    filt.first()
    cot.first_z()
    pl.semaphore_wait(gate, 7)
    cot.first_plane()
    filt.own_first()
    cot.own_first()
    filt.second()
    cot.second()
    feat.first_z()
    feat.first_plane()
    feat.own_first()
    filt.arrived()
    cot.arrived()
    input_part(cx, hx, taps_ref, tabs, oa, ob, spec_c, cs, hs, os, ds, bs, ys, zs)
    feat.second()
    grad.first_z()
    grad.first_plane()
    grad.own_first()
    feat.arrived()
    sums_part(ln, fx, cs, fs, sk)
    sums.first()
    filter_part(tabs, go, spec_c, fs, gs, ds, bs, ys, zs)
    fgrad.first()
    fgrad.own_first()
    sums.second()
    grad.second()
    fgrad.second()
    sums.third()
    for each_one in (filt, cot, feat, grad, fgrad):
        each_one.sent()
    grad.arrived()
    fgrad.arrived()
    sums.finish()


def run(feature, cotangent, long_filter, taps):
    def bf(*shape):
        return pltpu.VMEM(shape + (8, N), BF)

    def f32(*shape):
        return pltpu.VMEM(shape, F32)

    vm = pl.BlockSpec(memory_space=pltpu.VMEM)
    whole = pl.BlockSpec(memory_space=pl.ANY)
    return pl.pallas_call(
        kernel,
        out_shape=(
            jax.ShapeDtypeStruct((R, Z, V, 8, N), BF),
            jax.ShapeDtypeStruct((Z, V, 8, N), BF),
            jax.ShapeDtypeStruct((R, Z, 1, N), F32),
        ),
        in_specs=[whole] * 3 + [pl.BlockSpec(memory_space=pltpu.SMEM)] + [vm] * 6,
        out_specs=(vm, vm, vm),
        scratch_shapes=[
            bf(Z, 2, V), bf(R, V, Z), bf(Z, 2, V), bf(R, V, Z), bf(Z, 2, V), bf(R, V, Z),
            bf(Z, V), bf(Z, V), bf(R, Z, V), bf(R, Z, V), bf(Z, V),
            bf(Z, 2, V), bf(2, V, Z), bf(Z, V), bf(W, Z),
            f32(8, R * N, 2 * N), f32(W * Z * 8, N), f32(W * Z * 8, N), f32(V * Z * 8, N),
            f32(W * Z * 8, N), f32(V * Z * 8, N),
            pltpu.VMEM((N, 5 * N), BF), pltpu.VMEM((5 * N, 2 * N), BF),
            pltpu.VMEM((4 * N, 2 * N), BF), pltpu.VMEM((2 * N, 4 * N), BF),
            f32(1, N), f32(V, 1, N), f32(1, N), f32(Z, 1, N),
            pltpu.SemaphoreType.REGULAR,
            pltpu.SemaphoreType.DMA((19,)), pltpu.SemaphoreType.DMA((19,)), pltpu.SemaphoreType.DMA((3,)),
        ],
        compiler_params=pltpu.CompilerParams(
            collective_id=0, has_side_effects=True, vmem_limit_bytes=LIMIT << 20
        ),
    )(feature, cotangent, long_filter, taps, *tables(N))


def body(feature, cotangent, long_filter, short_filter, skip_gain):
    rep, grp, seq = lax.axis_index("rep"), lax.axis_index("grp"), lax.axis_index("seq")
    first = rep * 1024 + seq % Z * 128 + (grp * 4 + seq // Z) * 8
    taps = jnp.concatenate([short_filter, skip_gain[:, None]], 1)
    taps = lax.dynamic_slice_in_dim(taps, first, 8, 0)
    pairs = (2, 2, Z, V, 8, N)
    grad, filt, sums = run(
        feature.reshape(pairs), cotangent.reshape(pairs), long_filter.reshape(R, Z, V, 8, N), taps
    )
    return grad.reshape(1, -1, N), filt.reshape(-1, N).astype(F32), sums.reshape(-1)


def solution(mesh):
    return jax.shard_map(
        body,
        mesh=mesh,
        in_specs=(
            P("rep", None, ("grp", "seq")),
            P("rep", None, ("grp", "seq")),
            P(None, ("grp", "seq")),
            P(),
            P(),
        ),
        out_specs=(P("rep", None, ("grp", "seq")), P("rep", ("grp", "seq")), P()),
        check_vma=False,
    )
```
